128 devices in a mesh: pipe: 4 (over y), tensor: 8 (over x, core), dp: 4 (over z).
Axes of the slice: x: 4, y: 4, z: 4, core: 2. Of those that a mesh axis runs over, the one named last changes fastest.
Arguments:
- hidden: bfloat16 [16, 64, 16384], P('dp', None, ('pipe', 'tensor')), parts along dimension 0, may hold values from -200 to 200
- norm_gain: bfloat16 [16384], P(('pipe', 'tensor')), may hold values from 0.5 to 1.5
- head_weight: bfloat16 [16384, 24576], P(None, ('pipe', 'tensor')), may hold values from -0.5 to 0.5
Outputs:
- logits: bfloat16 [16, 64, 24576], P('dp', None, ('pipe', 'tensor')), parts along dimension 0
- probs: float32 [16, 64, 24576], P('dp', None, ('pipe', 'tensor')), parts along dimension 0
The draws below stay inside these ranges and needn't reach their ends.
There are 4 independent parts, one for each index of `dp`. The reference program is written for one: setup_inputs(seed, part) draws one part's arguments, and reference() takes and returns one part's arrays. A program takes and returns all parts, laid end to end along the dimension named above; an argument that names none is the same for every part. Nothing has to cross between parts.
All inputs are finite; a program needn't handle non-finite values.
Results may differ from the reference program's by a relative error of at most 0.012.
Values may be sent and summed in bfloat16 or wider, within the bound.
No kernel may reach another device: no remote copies, remote signals or barrier semaphores. Data moves between devices by JAX's collectives and lax.ppermute only.
A program may use at most 128 MiB of HBM per device.

```python
import math
import jax
import jax.numpy as jnp
from jax import lax

D = 16384
ROWS = 64
MICRO = 4
VOCAB = 24576


def draw_hidden(key, part):
    key = jax.random.fold_in(key, 11)
    first, second = jax.random.split(key)
    feature = 1.0 + 0.8 * jnp.arange(D, dtype=jnp.float32) / D
    row_scale = jnp.exp(jax.random.uniform(second, (MICRO, ROWS, 1), jnp.float32) * math.log(10.0))
    noise = jnp.clip(jax.random.normal(first, (MICRO, ROWS, D), jnp.float32), -5.0, 5.0)
    values = noise * feature * row_scale
    return jnp.clip(values, -200.0, 200.0).astype(jnp.bfloat16)


def draw_head_weight(key, part):
    key = jax.random.fold_in(key, 7)
    first, second = jax.random.split(key)
    column = jnp.arange(VOCAB, dtype=jnp.float32)
    spread = jnp.exp(jax.random.uniform(second, (VOCAB,), jnp.float32) * math.log(4.0))
    spread = spread * (1.0 + column / VOCAB) * 1.5 / math.sqrt(D)
    base = jnp.clip(jax.random.normal(first, (D, VOCAB), jnp.float32), -5.0, 5.0)
    weight = base * spread
    return jnp.clip(weight, -0.5, 0.5).astype(jnp.bfloat16)


def setup_inputs(seed: int = 0, part: int = 0) -> dict:
    arg_keys = jax.random.split(jax.random.key(seed), 4)
    own_keys = jax.random.split(jax.random.fold_in(arg_keys[3], part), 4)
    hidden = draw_hidden(jax.random.fold_in(jax.random.fold_in(arg_keys[3], part), 71), part)
    norm_gain = jnp.clip(1.0 + 0.1 * jax.random.normal(arg_keys[1], (D,), jnp.float32), 0.5, 1.5).astype(jnp.bfloat16)
    head_weight = draw_head_weight(jax.random.fold_in(arg_keys[3], 71), part)
    return {"hidden": hidden, "norm_gain": norm_gain, "head_weight": head_weight}


min_p_log = math.log(0.1)
gate_sharpness = 4.0

def reference(hidden, norm_gain, head_weight):
    values = hidden.astype(jnp.float32)
    mean_sq = lax.optimization_barrier(jnp.mean(jnp.square(values), axis=-1, keepdims=True))
    normed = (values * lax.rsqrt(mean_sq + 1e-05) * norm_gain.astype(jnp.float32)).astype(jnp.bfloat16)
    flat = normed.reshape(MICRO * ROWS, D)
    scores = jnp.dot(flat, head_weight, preferred_element_type=jnp.float32).reshape(MICRO, ROWS, VOCAB)
    top = lax.optimization_barrier(jnp.max(scores, axis=-1, keepdims=True))
    shifted = scores - top
    kept = jnp.exp(shifted) * jax.nn.sigmoid(gate_sharpness * (shifted - min_p_log))
    mass = lax.optimization_barrier(jnp.sum(kept, axis=-1, keepdims=True))
    return (scores.astype(jnp.bfloat16), kept / mass)
```

```python
import math

import jax
import jax.numpy as jnp
from jax import lax
from jax.experimental import pallas as pl
from jax.experimental.pallas import tpu as pltpu
from jax.sharding import PartitionSpec as P

AXES = ("pipe", "tensor")
PEERS = 32
LANES = 128
min_p_log = math.log(0.1)
gate_sharpness = 4.0
VMEM_LIMIT = 48 * 1024 * 1024


def exchange(values):
    return lax.all_to_all(values, AXES, 0, 0, tiled=True)


def spread_rows(column, out_ref):
    rows = column.shape[0]
    across = jnp.broadcast_to(column, (rows, LANES)).T
    for part in range(rows // LANES):
        out_ref[:, part, :] = across[: out_ref.shape[0], part * LANES : (part + 1) * LANES]


def rows_of(parts):
    across = jnp.concatenate(parts, axis=1)
    return jnp.broadcast_to(across, (LANES, across.shape[1])).T


def head_kernel(scale_ref, gain_ref, piece_ref, weight_ref, scores_ref, logits_ref, top_ref):
    step = pl.program_id(0)
    scale = scale_ref[...]
    normed = [
        (piece_ref[core].astype(jnp.float32) * scale * gain_ref[core].astype(jnp.float32)).astype(
            jnp.bfloat16
        )
        for core in range(2)
    ]
    term = jnp.dot(
        jnp.concatenate(normed, axis=1), weight_ref[...], preferred_element_type=jnp.float32
    )

    @pl.when(step == 0)
    def _():
        scores_ref[...] = term

    @pl.when(step > 0)
    def _():
        scores_ref[...] += term

    @pl.when(step == pl.num_programs(0) - 1)
    def _():
        scores = scores_ref[...]
        logits_ref[...] = scores.astype(jnp.bfloat16)
        spread_rows(jnp.max(scores, axis=1, keepdims=True), top_ref)


def head(pieces, scale, gain, weight):
    peers, rows, width = pieces.shape
    columns = weight.shape[1]
    return pl.pallas_call(
        head_kernel,
        grid=(peers // 2,),
        in_specs=[
            pl.BlockSpec((rows, 1), lambda i: (0, 0)),
            pl.BlockSpec((2, 1, width), lambda i: (i, 0, 0)),
            pl.BlockSpec((2, rows, width), lambda i: (i, 0, 0)),
            pl.BlockSpec((2 * width, columns), lambda i: (i, 0)),
        ],
        out_specs=[
            pl.BlockSpec((rows, columns), lambda i: (0, 0)),
            pl.BlockSpec((rows, columns), lambda i: (0, 0)),
            pl.BlockSpec((PEERS, 2, LANES), lambda i: (0, 0, 0)),
        ],
        out_shape=[
            jax.ShapeDtypeStruct((rows, columns), jnp.float32),
            jax.ShapeDtypeStruct((rows, columns), jnp.bfloat16),
            jax.ShapeDtypeStruct((PEERS, 2, LANES), jnp.float32),
        ],
        compiler_params=pltpu.CompilerParams(vmem_limit_bytes=VMEM_LIMIT),
        name="head",
    )(scale, gain, pieces, weight)


def gate_kernel(tops_ref, scores_ref, kept_ref, mass_ref):
    top = rows_of([jnp.max(tops_ref[:, part, :], axis=0, keepdims=True) for part in range(2)])
    shifted = scores_ref[...] - top[:, :1]
    kept = jnp.exp(shifted) * jax.nn.sigmoid(gate_sharpness * (shifted - min_p_log))
    kept_ref[...] = kept
    spread_rows(jnp.sum(kept, axis=1, keepdims=True), mass_ref)


def gate(tops, scores):
    return pl.pallas_call(
        gate_kernel,
        out_shape=[
            jax.ShapeDtypeStruct(scores.shape, jnp.float32),
            jax.ShapeDtypeStruct(tops.shape, jnp.float32),
        ],
        compiler_params=pltpu.CompilerParams(vmem_limit_bytes=VMEM_LIMIT),
        name="gate",
    )(tops, scores)


def share_kernel(masses_ref, kept_ref, probs_ref):
    mass = rows_of([jnp.sum(masses_ref[:, part, :], axis=0, keepdims=True) for part in range(2)])
    probs_ref[...] = kept_ref[...] / mass[:, :1]


def share(masses, kept):
    return pl.pallas_call(
        share_kernel,
        out_shape=jax.ShapeDtypeStruct(kept.shape, jnp.float32),
        compiler_params=pltpu.CompilerParams(vmem_limit_bytes=VMEM_LIMIT),
        name="share",
    )(masses, kept)


def local(hidden, norm_gain, head_weight):
    micro, rows, width = hidden.shape
    flat = hidden.reshape(micro * rows, width)
    pieces = lax.all_gather(flat, AXES, axis=0)

    local_sq = jnp.sum(jnp.square(flat.astype(jnp.float32)), axis=-1)
    note = jnp.concatenate([local_sq, norm_gain.astype(jnp.float32)]).reshape(-1, LANES)
    notes = exchange(jnp.broadcast_to(note[None], (PEERS,) + note.shape)).reshape(PEERS, -1)
    total_sq = jnp.sum(notes[:, : micro * rows], axis=0)
    scale = lax.rsqrt(total_sq / (width * PEERS) + 1e-05)[:, None]
    gain = notes[:, None, micro * rows :]

    scores, logits, tops = head(pieces, scale, gain, head_weight)
    kept, masses = gate(exchange(tops), scores)
    probs = share(exchange(masses), kept)
    shape = (micro, rows, head_weight.shape[1])
    return logits.reshape(shape), probs.reshape(shape)


def solution(mesh):
    return jax.shard_map(
        local,
        mesh=mesh,
        in_specs=(
            P("dp", None, AXES),
            P(AXES),
            P(None, AXES),
        ),
        out_specs=(P("dp", None, AXES), P("dp", None, AXES)),
        check_vma=False,
    )
```

```python
import functools
import math

import jax
import jax.numpy as jnp
from jax import lax
from jax.experimental import pallas as pl
from jax.experimental.pallas import tpu as pltpu
from jax.sharding import PartitionSpec as P

AXES = ("pipe", "tensor")
RING = 4
CORES = 2
PEERS = RING * RING * CORES
LANES = 128
NOTE = 16
HALF = 128
GROUP = 4
AHEAD = 4
min_p_log = math.log(0.1)
gate_sharpness = 4.0
HEAD_VMEM = 54 * 1024 * 1024
SMALL_VMEM = 8 * 1024 * 1024

WHOLE = NOTE + 2 * HALF
TOP = NOTE + HALF
ROW_CUT, COLUMN_CUT = 208, 192
PLACES = {
    (0, 0): [("own", 0), ("own", NOTE, 2 * HALF)],
    (0, -1): [("left", 0), ("left", NOTE, 2 * HALF)],
    (0, 1): [("right", 0), ("right", NOTE, 2 * HALF)],
    (-1, 0): [("down", 0), ("down", NOTE, 2 * HALF)],
    (1, 0): [("up", 0), ("up", NOTE, 2 * HALF)],
    (0, 2): [("cross_a", 0), ("cross_a", NOTE, HALF), ("cross_b", 0, HALF)],
    (2, 0): [("over_a", 0), ("over_a", NOTE, HALF), ("over_b", 0, HALF)],
}
for _dy, _array in ((-1, "row_down"), (1, "row_up")):
    for _at, _dx in enumerate((-1, 1, 2)):
        PLACES[_dy, _dx] = [(_array, _at * TOP), (_array, _at * TOP + NOTE, HALF)]
PLACES[2, -1] = [("far_down", 0), ("far_down", NOTE, HALF)]
PLACES[2, 1] = [
    ("far_down", TOP),
    ("far_down", TOP + NOTE, ROW_CUT - TOP - NOTE),
    ("far_up", 0, 2 * TOP - ROW_CUT),
]
PLACES[2, 2] = [("far_up", 2 * TOP - ROW_CUT), ("far_up", 2 * TOP - ROW_CUT + NOTE, HALF)]
for _dx, _array in ((-1, "col_left"), (1, "col_right")):
    for _at, _dy in enumerate((-1, 1, 2)):
        PLACES[_dy, _dx].append((_array, _at * HALF, HALF))
PLACES[-1, 2].append(("far_left", 0, HALF))
PLACES[1, 2] += [
    ("far_left", HALF, COLUMN_CUT - HALF),
    ("far_right", 0, 2 * HALF - COLUMN_CUT),
]
PLACES[2, 2].append(("far_right", 2 * HALF - COLUMN_CUT, HALF))


def device(y, x, core):
    return (y % RING) * RING * CORES + (x % RING) * CORES + core


def fetch(value, dy, dx, core=0):
    pairs = [
        (device(y + dy, x + dx, c ^ core), device(y, x, c))
        for y in range(RING)
        for x in range(RING)
        for c in range(CORES)
    ]
    return lax.ppermute(value, AXES, pairs)


def exchange(values):
    return lax.all_to_all(values, AXES, 0, 0, tiled=True)


def spread_rows(column, out_ref):
    rows = column.shape[0]
    across = jnp.broadcast_to(column, (rows, LANES)).T
    for part in range(rows // LANES):
        out_ref[:, part, :] = across[: out_ref.shape[0], part * LANES : (part + 1) * LANES]


def rows_of(parts):
    across = jnp.concatenate(parts, axis=1)
    return jnp.broadcast_to(across, (LANES, across.shape[1])).T


def head_kernel(keys, *refs):
    block_refs = dict(zip(keys, refs))
    weight_ref, scores_ref, logits_ref, top_ref = refs[len(keys) : len(keys) + 4]
    raw_ref, note_ref, normed_ref, part_ref, raw_sems, note_sems, sems = refs[len(keys) + 4 :]
    pipe, tensor = lax.axis_index("pipe"), lax.axis_index("tensor")
    chip_x, core = tensor // CORES, lax.rem(tensor, CORES)
    _, rows, width = raw_ref.shape
    terms = [(chip, which) for chip in PLACES for which in range(CORES)]
    groups = len(terms) // GROUP

    def shard(term):
        chip, which = terms[term]
        (note_array, note_at), *runs = PLACES[chip]
        copies = [
            pltpu.make_async_copy(
                block_refs[which, note_array].at[pl.ds(note_at, NOTE), :],
                note_ref.at[term],
                note_sems.at[term],
            )
        ]
        at = 0
        for i, (array, start, count) in enumerate(runs):
            copies.append(
                pltpu.make_async_copy(
                    block_refs[which, array].at[pl.ds(start, count), :],
                    raw_ref.at[term, pl.ds(at, count), :],
                    raw_sems.at[term, i],
                )
            )
            at += count
        return copies

    def weights(group):
        copies = []
        for i, term in enumerate(range(group * GROUP, (group + 1) * GROUP)):
            (dy, dx), which = terms[term]
            chip_at = lax.rem(pipe + dy + RING, RING) * RING + lax.rem(chip_x + dx + RING, RING)
            peer = chip_at * CORES + (core if which == 0 else 1 - core)
            copies.append(
                pltpu.make_async_copy(
                    weight_ref.at[pl.ds(pl.multiple_of(peer * width, width), width), :],
                    part_ref.at[group % AHEAD, pl.ds(i * width, width), :],
                    sems.at[group % AHEAD, i],
                )
            )
        return copies

    def fetch_weights(group):
        for copy in weights(group):
            copy.start()

    for term in range(len(terms)):
        for copy in shard(term):
            copy.start()
    for group in range(AHEAD - 1):
        fetch_weights(group)
    squares = jnp.zeros((rows, LANES), jnp.float32)
    for term in range(len(terms)):
        for copy in shard(term):
            copy.wait()
        for lane in range(0, width, LANES):
            squares += jnp.square(raw_ref[term, :, lane : lane + LANES].astype(jnp.float32))
    total_sq = jnp.sum(squares, axis=1, keepdims=True)
    scale = lax.rsqrt(total_sq / (width * len(terms)) + 1e-05)

    def norm(group):
        for i, term in enumerate(range(group * GROUP, (group + 1) * GROUP)):
            gain = note_ref[term].astype(jnp.float32)[:1]
            normed_ref[group % 2, :, i * width : (i + 1) * width] = (
                raw_ref[term].astype(jnp.float32) * scale * gain
            ).astype(jnp.bfloat16)

    norm(0)
    for group in range(groups):
        for copy in weights(group):
            copy.wait()
        if group + AHEAD - 1 < groups:
            fetch_weights(group + AHEAD - 1)
        term = jnp.dot(
            normed_ref[group % 2], part_ref[group % AHEAD], preferred_element_type=jnp.float32
        )
        if group + 1 < groups:
            norm(group + 1)
        if group == 0:
            scores_ref[...] = term
        elif group < groups - 1:
            scores_ref[...] += term
        else:
            scores = scores_ref[...] + term
            scores_ref[...] = scores
            logits_ref[...] = scores.astype(jnp.bfloat16)
            spread_rows(jnp.max(scores, axis=1, keepdims=True), top_ref)


def head(blocks, weight):
    names = dict.fromkeys(place[0] for places in PLACES.values() for place in places)
    keys = [(which, array) for which in range(CORES) for array in names]
    rows, columns = 2 * HALF, weight.shape[1]
    width = weight.shape[0] // PEERS
    in_vmem = pl.BlockSpec(memory_space=pltpu.VMEM)
    return pl.pallas_call(
        functools.partial(head_kernel, keys),
        in_specs=[pl.BlockSpec(memory_space=pl.ANY)] * (len(keys) + 1),
        out_specs=[in_vmem] * 3,
        out_shape=[
            jax.ShapeDtypeStruct((rows, columns), jnp.float32),
            jax.ShapeDtypeStruct((rows, columns), jnp.bfloat16),
            jax.ShapeDtypeStruct((PEERS, rows // LANES, LANES), jnp.float32),
        ],
        scratch_shapes=[
            pltpu.VMEM((PEERS, rows, width), jnp.bfloat16),
            pltpu.VMEM((PEERS, NOTE, width), jnp.bfloat16),
            pltpu.VMEM((2, rows, GROUP * width), jnp.bfloat16),
            pltpu.VMEM((AHEAD, GROUP * width, columns), jnp.bfloat16),
            pltpu.SemaphoreType.DMA((PEERS, 3)),
            pltpu.SemaphoreType.DMA((PEERS,)),
            pltpu.SemaphoreType.DMA((AHEAD, GROUP)),
        ],
        compiler_params=pltpu.CompilerParams(vmem_limit_bytes=HEAD_VMEM),
        name="head",
    )(*[blocks[key] for key in keys], weight)


def gate_kernel(tops_ref, scores_ref, kept_ref, mass_ref):
    parts = tops_ref.shape[1]
    top = rows_of([jnp.max(tops_ref[:, part, :], axis=0, keepdims=True) for part in range(parts)])
    shifted = scores_ref[...] - top[:, :1]
    kept = jnp.exp(shifted) * jax.nn.sigmoid(gate_sharpness * (shifted - min_p_log))
    kept_ref[...] = kept
    spread_rows(jnp.sum(kept, axis=1, keepdims=True), mass_ref)


def gate(tops, scores):
    return pl.pallas_call(
        gate_kernel,
        out_shape=[
            jax.ShapeDtypeStruct(scores.shape, jnp.float32),
            jax.ShapeDtypeStruct(tops.shape, jnp.float32),
        ],
        compiler_params=pltpu.CompilerParams(vmem_limit_bytes=SMALL_VMEM),
        name="gate",
    )(tops, scores)


def share_kernel(masses_ref, kept_ref, probs_ref):
    parts = masses_ref.shape[1]
    mass = rows_of(
        [jnp.sum(masses_ref[:, part, :], axis=0, keepdims=True) for part in range(parts)]
    )
    probs_ref[...] = kept_ref[...] / mass[:, :1]


def share(masses, kept):
    return pl.pallas_call(
        share_kernel,
        out_shape=jax.ShapeDtypeStruct(kept.shape, jnp.float32),
        compiler_params=pltpu.CompilerParams(vmem_limit_bytes=SMALL_VMEM),
        name="share",
    )(masses, kept)


def local(hidden, norm_gain, head_weight):
    micro, rows, width = hidden.shape
    blocks = {}

    def keep(name, value):
        blocks[0, name] = value
        blocks[1, name] = fetch(value, 0, 0, 1)
        return value

    note = jnp.pad(norm_gain[None], ((0, NOTE - 1), (0, 0)))
    own = keep("own", jnp.concatenate([note, hidden.reshape(micro * rows, width)], axis=0))
    left, right = keep("left", fetch(own, 0, -1)), keep("right", fetch(own, 0, 1))
    down, up = keep("down", fetch(own, -1, 0)), keep("up", fetch(own, 1, 0))
    cross_a = keep("cross_a", fetch(left[:TOP], 0, -1))
    cross_b = keep("cross_b", fetch(right[TOP:], 0, 1))
    over_a = keep("over_a", fetch(down[:TOP], -1, 0))
    over_b = keep("over_b", fetch(up[TOP:], 1, 0))

    row = jnp.concatenate([left[:TOP], right[:TOP], cross_a], axis=0)
    column = jnp.concatenate([down[TOP:], up[TOP:], over_b], axis=0)
    row, column, cross_b, over_a = lax.optimization_barrier((row, column, cross_b, over_a))
    row_down, row_up = keep("row_down", fetch(row, -1, 0)), keep("row_up", fetch(row, 1, 0))
    col_left, col_right = (
        keep("col_left", fetch(column, 0, -1)),
        keep("col_right", fetch(column, 0, 1)),
    )
    keep("far_down", fetch(row_down[:ROW_CUT], -1, 0))
    keep("far_up", fetch(row_up[ROW_CUT:], 1, 0))
    keep("far_left", fetch(col_left[:COLUMN_CUT], 0, -1))
    keep("far_right", fetch(col_right[COLUMN_CUT:], 0, 1))
    scores, logits, tops = head(blocks, head_weight)

    kept, masses = gate(exchange(tops), scores)
    probs = share(exchange(masses), kept)
    shape = (micro, rows, head_weight.shape[1])
    return logits.reshape(shape), probs.reshape(shape)


def solution(mesh):
    return jax.shard_map(
        local,
        mesh=mesh,
        in_specs=(
            P("dp", None, AXES),
            P(AXES),
            P(None, AXES),
        ),
        out_specs=(P("dp", None, AXES), P("dp", None, AXES)),
        check_vma=False,
    )
```

```python
import functools
import math

import jax
import jax.numpy as jnp
from jax import lax
from jax.experimental import pallas as pl
from jax.experimental.pallas import tpu as pltpu
from jax.sharding import PartitionSpec as P

AXES = ("pipe", "tensor")
RING = 4
CORES = 2
PEERS = RING * RING * CORES
LANES = 128
NOTE = 16
HALF = 128
GROUP = 4
min_p_log = math.log(0.1)
gate_sharpness = 4.0
HEAD_VMEM = 14 * 1024 * 1024
SMALL_VMEM = 8 * 1024 * 1024

WHOLE = NOTE + 2 * HALF
TOP = NOTE + HALF
PLACES = {
    (0, 0): [("own", 0), ("own", NOTE, 2 * HALF)],
    (0, -1): [("left", 0), ("left", NOTE, 2 * HALF)],
    (0, 1): [("right", 0), ("right", NOTE, 2 * HALF)],
    (-1, 0): [("down", 0), ("down", NOTE, 2 * HALF)],
    (1, 0): [("up", 0), ("up", NOTE, 2 * HALF)],
    (0, 2): [("cross", 0), ("cross", NOTE, 2 * HALF)],
    (2, 0): [("over", 0), ("over", NOTE, 2 * HALF)],
}
for _dy, _array in ((-1, "row_down"), (1, "row_up"), (2, "row_over")):
    for _at, _dx in enumerate((-1, 1, 2)):
        PLACES[_dy, _dx] = [(_array, _at * TOP), (_array, _at * TOP + NOTE, HALF)]
for _dx, _array in ((-1, "col_left"), (1, "col_right"), (2, "col_cross")):
    for _at, _dy in enumerate((-1, 1, 2)):
        PLACES[_dy, _dx].append((_array, _at * HALF, HALF))


def device(y, x, core):
    return (y % RING) * RING * CORES + (x % RING) * CORES + core


def fetch(value, dy, dx, core=0):
    pairs = [
        (device(y + dy, x + dx, c ^ core), device(y, x, c))
        for y in range(RING)
        for x in range(RING)
        for c in range(CORES)
    ]
    return lax.ppermute(value, AXES, pairs)


def exchange(values):
    return lax.all_to_all(values, AXES, 0, 0, tiled=True)


def spread_rows(column, out_ref):
    rows = column.shape[0]
    across = jnp.broadcast_to(column, (rows, LANES)).T
    for part in range(rows // LANES):
        out_ref[:, part, :] = across[: out_ref.shape[0], part * LANES : (part + 1) * LANES]


def rows_of(parts):
    across = jnp.concatenate(parts, axis=1)
    return jnp.broadcast_to(across, (LANES, across.shape[1])).T


def bring(weight):
    def kernel(weight_ref, out_ref, sem):
        copy = pltpu.make_async_copy(weight_ref, out_ref, sem)
        copy.start()
        copy.wait()

    return pl.pallas_call(
        kernel,
        in_specs=[pl.BlockSpec(memory_space=pl.ANY)],
        out_specs=pl.BlockSpec(memory_space=pltpu.VMEM),
        out_shape=jax.ShapeDtypeStruct(weight.shape, weight.dtype),
        scratch_shapes=[pltpu.SemaphoreType.DMA],
        compiler_params=pltpu.CompilerParams(vmem_limit_bytes=SMALL_VMEM),
        cost_estimate=pl.CostEstimate(
            flops=0, bytes_accessed=2 * weight.size * weight.dtype.itemsize, transcendentals=0
        ),
        name="bring",
    )(weight)


def head_kernel(keys, *refs):
    block_refs = dict(zip(keys, refs))
    weight_ref, scores_ref, logits_ref, top_ref, normed_ref = refs[len(keys) :]
    pipe, tensor = lax.axis_index("pipe"), lax.axis_index("tensor")
    chip_x, core = tensor // CORES, lax.rem(tensor, CORES)
    rows = scores_ref.shape[0]
    width = weight_ref.shape[0] // PEERS
    terms = [(chip, which) for chip in PLACES for which in range(CORES)]
    groups = len(terms) // GROUP

    def runs(term):
        chip, which = terms[term]
        at = 0
        for array, start, count in PLACES[chip][1:]:
            yield slice(at, at + count), block_refs[which, array].at[pl.ds(start, count), :]
            at += count

    def gain_of(term):
        chip, which = terms[term]
        array, start = PLACES[chip][0]
        return block_refs[which, array][start : start + NOTE, :].astype(jnp.float32)[:1]

    squares = []
    for half in range(2):
        total = jnp.zeros((HALF, LANES), jnp.float32)
        for term in range(len(terms)):
            parts = []
            for at, ref in runs(term):
                first, last = max(at.start, half * HALF), min(at.stop, (half + 1) * HALF)
                if first < last:
                    parts.append(
                        sum(
                            jnp.square(
                                ref[
                                    first - at.start : last - at.start, lane : lane + LANES
                                ].astype(jnp.float32)
                            )
                            for lane in range(0, width, LANES)
                        )
                    )
            total += parts[0] if len(parts) == 1 else jnp.concatenate(parts, axis=0)
        squares.append(jnp.sum(total, axis=1, keepdims=True))
    total_sq = jnp.concatenate(squares, axis=0)
    scale = lax.rsqrt(total_sq / (width * len(terms)) + 1e-05)

    def norm(group):
        for i, term in enumerate(range(group * GROUP, (group + 1) * GROUP)):
            gain = gain_of(term)
            for at, ref in runs(term):
                normed_ref[group % 2, at, i * width : (i + 1) * width] = (
                    ref[...].astype(jnp.float32) * scale[at] * gain
                ).astype(jnp.bfloat16)

    def product(group):
        total = None
        for i in range(0, GROUP):
            (dy, dx), which = terms[group * GROUP + i]
            chip_at = lax.rem(pipe + dy + RING, RING) * RING + lax.rem(chip_x + dx + RING, RING)
            peer = chip_at * CORES + (core if which == 0 else 1 - core)
            term = jnp.dot(
                normed_ref[group % 2, :, i * width : (i + 1) * width],
                weight_ref[pl.ds(pl.multiple_of(peer * width, width), width), :],
                preferred_element_type=jnp.float32,
            )
            total = term if total is None else total + term
        return total

    norm(0)
    for group in range(groups):
        term = product(group)
        if group + 1 < groups:
            norm(group + 1)
        if group == 0:
            scores_ref[...] = term
        elif group < groups - 1:
            scores_ref[...] += term
        else:
            scores = scores_ref[...] + term
            scores_ref[...] = scores
            logits_ref[...] = scores.astype(jnp.bfloat16)
            spread_rows(jnp.max(scores, axis=1, keepdims=True), top_ref)


def head(blocks, weight):
    names = dict.fromkeys(place[0] for places in PLACES.values() for place in places)
    keys = [(which, array) for which in range(CORES) for array in names]
    rows, columns = 2 * HALF, weight.shape[1]
    width = weight.shape[0] // PEERS
    in_vmem = pl.BlockSpec(memory_space=pltpu.VMEM)
    return pl.pallas_call(
        functools.partial(head_kernel, keys),
        in_specs=[in_vmem] * (len(keys) + 1),
        out_specs=[in_vmem] * 3,
        out_shape=[
            jax.ShapeDtypeStruct((rows, columns), jnp.float32),
            jax.ShapeDtypeStruct((rows, columns), jnp.bfloat16),
            jax.ShapeDtypeStruct((PEERS, rows // LANES, LANES), jnp.float32),
        ],
        scratch_shapes=[pltpu.VMEM((2, rows, GROUP * width), jnp.bfloat16)],
        compiler_params=pltpu.CompilerParams(vmem_limit_bytes=HEAD_VMEM),
        name="head",
    )(*[blocks[key] for key in keys], weight)


def gate_kernel(tops_ref, scores_ref, kept_ref, mass_ref):
    parts = tops_ref.shape[1]
    top = rows_of([jnp.max(tops_ref[:, part, :], axis=0, keepdims=True) for part in range(parts)])
    shifted = scores_ref[...] - top[:, :1]
    kept = jnp.exp(shifted) * jax.nn.sigmoid(gate_sharpness * (shifted - min_p_log))
    kept_ref[...] = kept
    spread_rows(jnp.sum(kept, axis=1, keepdims=True), mass_ref)


def gate(tops, scores):
    return pl.pallas_call(
        gate_kernel,
        out_shape=[
            jax.ShapeDtypeStruct(scores.shape, jnp.float32),
            jax.ShapeDtypeStruct(tops.shape, jnp.float32),
        ],
        compiler_params=pltpu.CompilerParams(vmem_limit_bytes=SMALL_VMEM),
        name="gate",
    )(tops, scores)


def share_kernel(masses_ref, kept_ref, probs_ref):
    parts = masses_ref.shape[1]
    mass = rows_of(
        [jnp.sum(masses_ref[:, part, :], axis=0, keepdims=True) for part in range(parts)]
    )
    probs_ref[...] = kept_ref[...] / mass[:, :1]


def share(masses, kept):
    return pl.pallas_call(
        share_kernel,
        out_shape=jax.ShapeDtypeStruct(kept.shape, jnp.float32),
        compiler_params=pltpu.CompilerParams(vmem_limit_bytes=SMALL_VMEM),
        name="share",
    )(masses, kept)


def local(hidden, norm_gain, head_weight):
    micro, rows, width = hidden.shape
    blocks = {}

    def keep(name, value):
        blocks[0, name] = value
        blocks[1, name] = fetch(value, 0, 0, 1)
        return value

    note = jnp.pad(norm_gain[None], ((0, NOTE - 1), (0, 0)))
    own = keep("own", jnp.concatenate([note, hidden.reshape(micro * rows, width)], axis=0))
    left, right = keep("left", fetch(own, 0, -1)), keep("right", fetch(own, 0, 1))
    down, up = keep("down", fetch(own, -1, 0)), keep("up", fetch(own, 1, 0))
    cross, over = keep("cross", fetch(own, 0, 2)), keep("over", fetch(own, 2, 0))

    row = jnp.concatenate([left[:TOP], right[:TOP], cross[:TOP]], axis=0)
    column = jnp.concatenate([down[TOP:], up[TOP:], over[TOP:]], axis=0)
    row_down, row_up = keep("row_down", fetch(row, -1, 0)), keep("row_up", fetch(row, 1, 0))
    col_left, col_right = (
        keep("col_left", fetch(column, 0, -1)),
        keep("col_right", fetch(column, 0, 1)),
    )
    keep("row_over", fetch(row, 2, 0))
    keep("col_cross", fetch(column, 0, 2))
    scores, logits, tops = head(blocks, bring(head_weight))

    kept, masses = gate(exchange(tops), scores)
    probs = share(exchange(masses), kept)
    shape = (micro, rows, head_weight.shape[1])
    return logits.reshape(shape), probs.reshape(shape)


def solution(mesh):
    return jax.shard_map(
        local,
        mesh=mesh,
        in_specs=(
            P("dp", None, AXES),
            P(AXES),
            P(None, AXES),
        ),
        out_specs=(P("dp", None, AXES), P("dp", None, AXES)),
        check_vma=False,
    )
```

```python
import functools
import math

import jax
import jax.numpy as jnp
from jax import lax
from jax.experimental import pallas as pl
from jax.experimental.pallas import tpu as pltpu
from jax.sharding import PartitionSpec as P

AXES = ("pipe", "tensor")
RING = 4
CORES = 2
PEERS = RING * RING * CORES
LANES = 128
NOTE = 16
HALF = 128
GROUP = 4
min_p_log = math.log(0.1)
gate_sharpness = 4.0
HEAD_VMEM = 14 * 1024 * 1024
SMALL_VMEM = 8 * 1024 * 1024

WHOLE = NOTE + 2 * HALF
TOP = NOTE + HALF
PLACES = {
    (0, 0): [("own", 0), ("own", NOTE, 2 * HALF)],
    (0, -1): [("left", 0), ("left", NOTE, 2 * HALF)],
    (0, 1): [("right", 0), ("right", NOTE, 2 * HALF)],
    (-1, 0): [("down", 0), ("down", NOTE, 2 * HALF)],
    (1, 0): [("up", 0), ("up", NOTE, 2 * HALF)],
    (0, 2): [("cross", 0), ("cross", NOTE, 2 * HALF)],
    (2, 0): [("over", 0), ("over", NOTE, 2 * HALF)],
}
for _dy, _array in ((-1, "row_down"), (1, "row_up"), (2, "row_over")):
    for _at, _dx in enumerate((-1, 1, 2)):
        PLACES[_dy, _dx] = [(_array, _at * TOP), (_array, _at * TOP + NOTE, HALF)]
for _dx, _array in ((-1, "col_left"), (1, "col_right"), (2, "col_cross")):
    for _at, _dy in enumerate((-1, 1, 2)):
        PLACES[_dy, _dx].append((_array, _at * HALF, HALF))


def device(y, x, core):
    return (y % RING) * RING * CORES + (x % RING) * CORES + core


def fetch(value, dy, dx, core=0):
    pairs = [
        (device(y + dy, x + dx, c ^ core), device(y, x, c))
        for y in range(RING)
        for x in range(RING)
        for c in range(CORES)
    ]
    return lax.ppermute(value, AXES, pairs)


def exchange(values):
    return lax.all_to_all(values, AXES, 0, 0, tiled=True)


def spread_rows(column, out_ref):
    rows = column.shape[0]
    across = jnp.broadcast_to(column, (rows, LANES)).T
    for part in range(rows // LANES):
        out_ref[:, part, :] = across[: out_ref.shape[0], part * LANES : (part + 1) * LANES]


def rows_of(parts):
    across = jnp.concatenate(parts, axis=1)
    return jnp.broadcast_to(across, (LANES, across.shape[1])).T


def join(pieces):
    counts = [piece.shape[0] for piece in pieces]

    def kernel(*refs):
        at = 0
        for ref, count in zip(refs, counts):
            refs[-1][at : at + count, :] = ref[...]
            at += count

    return pl.pallas_call(
        kernel,
        in_specs=[pl.BlockSpec(memory_space=pltpu.VMEM)] * len(pieces),
        out_specs=pl.BlockSpec(memory_space=pltpu.VMEM),
        out_shape=jax.ShapeDtypeStruct((sum(counts), pieces[0].shape[1]), pieces[0].dtype),
        compiler_params=pltpu.CompilerParams(vmem_limit_bytes=SMALL_VMEM),
        cost_estimate=pl.CostEstimate(flops=13800000000, bytes_accessed=0, transcendentals=0),
        name="join",
    )(*pieces)


def head_kernel(keys, *refs):
    block_refs = dict(zip(keys, refs))
    weight_ref, scores_ref, logits_ref, top_ref, normed_ref = refs[len(keys) :]
    pipe, tensor = lax.axis_index("pipe"), lax.axis_index("tensor")
    chip_x, core = tensor // CORES, lax.rem(tensor, CORES)
    rows = scores_ref.shape[0]
    width = weight_ref.shape[0] // PEERS
    terms = [(chip, which) for chip in PLACES for which in range(CORES)]
    groups = len(terms) // GROUP

    def runs(term):
        chip, which = terms[term]
        at = 0
        for array, start, count in PLACES[chip][1:]:
            yield slice(at, at + count), block_refs[which, array].at[pl.ds(start, count), :]
            at += count

    def gain_of(term):
        chip, which = terms[term]
        array, start = PLACES[chip][0]
        return block_refs[which, array][start : start + NOTE, :].astype(jnp.float32)[:1]

    squares = []
    for half in range(2):
        total = jnp.zeros((HALF, LANES), jnp.float32)
        for term in range(len(terms)):
            parts = []
            for at, ref in runs(term):
                first, last = max(at.start, half * HALF), min(at.stop, (half + 1) * HALF)
                if first < last:
                    parts.append(
                        sum(
                            jnp.square(
                                ref[
                                    first - at.start : last - at.start, lane : lane + LANES
                                ].astype(jnp.float32)
                            )
                            for lane in range(0, width, LANES)
                        )
                    )
            total += parts[0] if len(parts) == 1 else jnp.concatenate(parts, axis=0)
        squares.append(jnp.sum(total, axis=1, keepdims=True))
    total_sq = jnp.concatenate(squares, axis=0)
    scale = lax.rsqrt(total_sq / (width * len(terms)) + 1e-05)

    def norm(group):
        for i, term in enumerate(range(group * GROUP, (group + 1) * GROUP)):
            gain = gain_of(term)
            for at, ref in runs(term):
                normed_ref[group % 2, at, i * width : (i + 1) * width] = (
                    ref[...].astype(jnp.float32) * scale[at] * gain
                ).astype(jnp.bfloat16)

    def product(group):
        total = None
        for i in range(0, GROUP):
            (dy, dx), which = terms[group * GROUP + i]
            chip_at = lax.rem(pipe + dy + RING, RING) * RING + lax.rem(chip_x + dx + RING, RING)
            peer = chip_at * CORES + (core if which == 0 else 1 - core)
            term = jnp.dot(
                normed_ref[group % 2, :, i * width : (i + 1) * width],
                weight_ref[pl.ds(pl.multiple_of(peer * width, width), width), :],
                preferred_element_type=jnp.float32,
            )
            total = term if total is None else total + term
        return total

    norm(0)
    for group in range(groups):
        term = product(group)
        if group + 1 < groups:
            norm(group + 1)
        if group == 0:
            scores_ref[...] = term
        elif group < groups - 1:
            scores_ref[...] += term
        else:
            scores = scores_ref[...] + term
            scores_ref[...] = scores
            logits_ref[...] = scores.astype(jnp.bfloat16)
            spread_rows(jnp.max(scores, axis=1, keepdims=True), top_ref)


def head(blocks, weight):
    names = dict.fromkeys(place[0] for places in PLACES.values() for place in places)
    keys = [(which, array) for which in range(CORES) for array in names]
    rows, columns = 2 * HALF, weight.shape[1]
    width = weight.shape[0] // PEERS
    in_vmem = pl.BlockSpec(memory_space=pltpu.VMEM)
    return pl.pallas_call(
        functools.partial(head_kernel, keys),
        in_specs=[in_vmem] * (len(keys) + 1),
        out_specs=[in_vmem] * 3,
        out_shape=[
            jax.ShapeDtypeStruct((rows, columns), jnp.float32),
            jax.ShapeDtypeStruct((rows, columns), jnp.bfloat16),
            jax.ShapeDtypeStruct((PEERS, rows // LANES, LANES), jnp.float32),
        ],
        scratch_shapes=[pltpu.VMEM((2, rows, GROUP * width), jnp.bfloat16)],
        compiler_params=pltpu.CompilerParams(vmem_limit_bytes=HEAD_VMEM),
        name="head",
    )(*[blocks[key] for key in keys], weight)


def gate_kernel(tops_ref, scores_ref, kept_ref, mass_ref):
    parts = tops_ref.shape[1]
    top = rows_of([jnp.max(tops_ref[:, part, :], axis=0, keepdims=True) for part in range(parts)])
    shifted = scores_ref[...] - top[:, :1]
    kept = jnp.exp(shifted) * jax.nn.sigmoid(gate_sharpness * (shifted - min_p_log))
    kept_ref[...] = kept
    spread_rows(jnp.sum(kept, axis=1, keepdims=True), mass_ref)


def gate(tops, scores):
    return pl.pallas_call(
        gate_kernel,
        out_shape=[
            jax.ShapeDtypeStruct(scores.shape, jnp.float32),
            jax.ShapeDtypeStruct(tops.shape, jnp.float32),
        ],
        compiler_params=pltpu.CompilerParams(vmem_limit_bytes=SMALL_VMEM),
        name="gate",
    )(tops, scores)


def share_kernel(masses_ref, kept_ref, probs_ref):
    parts = masses_ref.shape[1]
    mass = rows_of(
        [jnp.sum(masses_ref[:, part, :], axis=0, keepdims=True) for part in range(parts)]
    )
    probs_ref[...] = kept_ref[...] / mass[:, :1]


def share(masses, kept):
    return pl.pallas_call(
        share_kernel,
        out_shape=jax.ShapeDtypeStruct(kept.shape, jnp.float32),
        compiler_params=pltpu.CompilerParams(vmem_limit_bytes=SMALL_VMEM),
        name="share",
    )(masses, kept)


def local(hidden, norm_gain, head_weight):
    micro, rows, width = hidden.shape
    blocks = {}

    def keep(name, value):
        blocks[0, name] = value
        blocks[1, name] = fetch(value, 0, 0, 1)
        return value

    note = jnp.pad(norm_gain[None], ((0, NOTE - 1), (0, 0)))
    own = keep("own", jnp.concatenate([note, hidden.reshape(micro * rows, width)], axis=0))
    left, right = keep("left", fetch(own, 0, -1)), keep("right", fetch(own, 0, 1))
    down, up = keep("down", fetch(own, -1, 0)), keep("up", fetch(own, 1, 0))
    cross, over = keep("cross", fetch(own, 0, 2)), keep("over", fetch(own, 2, 0))

    row = join([left[:TOP], right[:TOP], cross[:TOP]])
    column = jnp.concatenate([down[TOP:], up[TOP:], over[TOP:]], axis=0)
    row_down, row_up = keep("row_down", fetch(row, -1, 0)), keep("row_up", fetch(row, 1, 0))
    col_left, col_right = (
        keep("col_left", fetch(column, 0, -1)),
        keep("col_right", fetch(column, 0, 1)),
    )
    keep("row_over", fetch(row, 2, 0))
    keep("col_cross", fetch(column, 0, 2))
    scores, logits, tops = head(blocks, head_weight)

    kept, masses = gate(exchange(tops), scores)
    probs = share(exchange(masses), kept)
    shape = (micro, rows, head_weight.shape[1])
    return logits.reshape(shape), probs.reshape(shape)


def solution(mesh):
    return jax.shard_map(
        local,
        mesh=mesh,
        in_specs=(
            P("dp", None, AXES),
            P(AXES),
            P(None, AXES),
        ),
        out_specs=(P("dp", None, AXES), P("dp", None, AXES)),
        check_vma=False,
    )
```

```python
import functools
import math

import jax
import jax.numpy as jnp
from jax import lax
from jax.experimental import pallas as pl
from jax.experimental.pallas import tpu as pltpu
from jax.sharding import PartitionSpec as P

AXES = ("pipe", "tensor")
RING = 4
CORES = 2
PEERS = RING * RING * CORES
LANES = 128
NOTE = 16
HALF = 128
GROUP = 4
min_p_log = math.log(0.1)
gate_sharpness = 4.0
HEAD_VMEM = 14 * 1024 * 1024
SMALL_VMEM = 8 * 1024 * 1024

WHOLE = NOTE + 2 * HALF
TOP = NOTE + HALF
PLACES = {
    (0, 0): [("own", 0), ("own", NOTE, 2 * HALF)],
    (0, -1): [("left", 0), ("left", NOTE, 2 * HALF)],
    (0, 1): [("right", 0), ("right", NOTE, 2 * HALF)],
    (-1, 0): [("down", 0), ("down", NOTE, 2 * HALF)],
    (1, 0): [("up", 0), ("up", NOTE, 2 * HALF)],
    (0, 2): [("cross", 0), ("cross", NOTE, 2 * HALF)],
    (2, 0): [("over", 0), ("over", NOTE, 2 * HALF)],
}
for _dy, _array in ((-1, "row_down"), (1, "row_up"), (2, "row_over")):
    for _at, _dx in enumerate((-1, 1, 2)):
        PLACES[_dy, _dx] = [(_array, _at * TOP), (_array, _at * TOP + NOTE, HALF)]
for _dx, _array in ((-1, "col_left"), (1, "col_right"), (2, "col_cross")):
    for _at, _dy in enumerate((-1, 1, 2)):
        PLACES[_dy, _dx].append((_array, _at * HALF, HALF))


def device(y, x, core):
    return (y % RING) * RING * CORES + (x % RING) * CORES + core


def fetch(value, dy, dx, core=0):
    pairs = [
        (device(y + dy, x + dx, c ^ core), device(y, x, c))
        for y in range(RING)
        for x in range(RING)
        for c in range(CORES)
    ]
    return lax.ppermute(value, AXES, pairs)


def exchange(values):
    return lax.all_to_all(values, AXES, 0, 0, tiled=True)


def spread_rows(column, out_ref):
    rows = column.shape[0]
    across = jnp.broadcast_to(column, (rows, LANES)).T
    for part in range(rows // LANES):
        out_ref[:, part, :] = across[: out_ref.shape[0], part * LANES : (part + 1) * LANES]


def rows_of(parts):
    across = jnp.concatenate(parts, axis=1)
    return jnp.broadcast_to(across, (LANES, across.shape[1])).T


def join(pieces):
    counts = [piece.shape[0] for piece in pieces]

    def kernel(*refs):
        at = 0
        for ref, count in zip(refs, counts):
            refs[-1][at : at + count, :] = ref[...]
            at += count

    return pl.pallas_call(
        kernel,
        in_specs=[pl.BlockSpec(memory_space=pltpu.VMEM)] * len(pieces),
        out_specs=pl.BlockSpec(memory_space=pltpu.VMEM),
        out_shape=jax.ShapeDtypeStruct((sum(counts), pieces[0].shape[1]), pieces[0].dtype),
        compiler_params=pltpu.CompilerParams(vmem_limit_bytes=SMALL_VMEM),
        cost_estimate=pl.CostEstimate(flops=13800000000, bytes_accessed=0, transcendentals=0),
        name="join",
    )(*pieces)


def runs_of(term, block_refs):
    chip, which = term
    at = 0
    for array, start, count in PLACES[chip][1:]:
        yield slice(at, at + count), block_refs[which, array].at[pl.ds(start, count), :]
        at += count


def early(term):
    chip, which = term
    return which == 0 or 0 in chip


def add_squares(terms, block_refs):
    halves = []
    for half in range(2):
        total = jnp.zeros((HALF, LANES), jnp.float32)
        for term in terms:
            parts = []
            for at, ref in runs_of(term, block_refs):
                first, last = max(at.start, half * HALF), min(at.stop, (half + 1) * HALF)
                if first < last:
                    parts.append(
                        sum(
                            jnp.square(
                                ref[
                                    first - at.start : last - at.start, lane : lane + LANES
                                ].astype(jnp.float32)
                            )
                            for lane in range(0, ref.shape[1], LANES)
                        )
                    )
            total += parts[0] if len(parts) == 1 else jnp.concatenate(parts, axis=0)
        halves.append(total)
    return jnp.concatenate(halves, axis=0)


def early_squares(blocks):
    terms = [(chip, which) for chip in PLACES for which in range(CORES) if early((chip, which))]
    keys = list(
        dict.fromkeys((which, place[0]) for chip, which in terms for place in PLACES[chip])
    )

    def kernel(*refs):
        refs[-1][...] = add_squares(terms, dict(zip(keys, refs)))

    return pl.pallas_call(
        kernel,
        in_specs=[pl.BlockSpec(memory_space=pltpu.VMEM)] * len(keys),
        out_specs=pl.BlockSpec(memory_space=pltpu.VMEM),
        out_shape=jax.ShapeDtypeStruct((2 * HALF, LANES), jnp.float32),
        compiler_params=pltpu.CompilerParams(vmem_limit_bytes=SMALL_VMEM),
        name="early_squares",
    )(*[blocks[key] for key in keys])


def head_kernel(keys, *refs):
    block_refs = dict(zip(keys, refs))
    squares_ref, weight_ref, scores_ref, logits_ref, top_ref, normed_ref = refs[len(keys) :]
    pipe, tensor = lax.axis_index("pipe"), lax.axis_index("tensor")
    chip_x, core = tensor // CORES, lax.rem(tensor, CORES)
    rows = scores_ref.shape[0]
    width = weight_ref.shape[0] // PEERS
    terms = [(chip, which) for chip in PLACES for which in range(CORES)]
    groups = len(terms) // GROUP

    def gain_of(term):
        chip, which = terms[term]
        array, start = PLACES[chip][0]
        return block_refs[which, array][start : start + NOTE, :].astype(jnp.float32)[:1]

    late = [term for term in terms if not early(term)]
    total_sq = jnp.sum(squares_ref[...] + add_squares(late, block_refs), axis=1, keepdims=True)
    scale = lax.rsqrt(total_sq / (width * len(terms)) + 1e-05)

    def norm(group):
        for i, term in enumerate(range(group * GROUP, (group + 1) * GROUP)):
            gain = gain_of(term)
            for at, ref in runs_of(terms[term], block_refs):
                normed_ref[group % 2, at, i * width : (i + 1) * width] = (
                    ref[...].astype(jnp.float32) * scale[at] * gain
                ).astype(jnp.bfloat16)

    def product(group):
        total = None
        for i in range(0, GROUP):
            (dy, dx), which = terms[group * GROUP + i]
            chip_at = lax.rem(pipe + dy + RING, RING) * RING + lax.rem(chip_x + dx + RING, RING)
            peer = chip_at * CORES + (core if which == 0 else 1 - core)
            term = jnp.dot(
                normed_ref[group % 2, :, i * width : (i + 1) * width],
                weight_ref[pl.ds(pl.multiple_of(peer * width, width), width), :],
                preferred_element_type=jnp.float32,
            )
            total = term if total is None else total + term
        return total

    norm(0)
    for group in range(groups):
        term = product(group)
        if group + 1 < groups:
            norm(group + 1)
        if group == 0:
            scores_ref[...] = term
        elif group < groups - 1:
            scores_ref[...] += term
        else:
            scores = scores_ref[...] + term
            scores_ref[...] = scores
            logits_ref[...] = scores.astype(jnp.bfloat16)
            spread_rows(jnp.max(scores, axis=1, keepdims=True), top_ref)


def head(blocks, weight):
    names = dict.fromkeys(place[0] for places in PLACES.values() for place in places)
    keys = [(which, array) for which in range(CORES) for array in names]
    rows, columns = 2 * HALF, weight.shape[1]
    width = weight.shape[0] // PEERS
    in_vmem = pl.BlockSpec(memory_space=pltpu.VMEM)
    return pl.pallas_call(
        functools.partial(head_kernel, keys),
        in_specs=[in_vmem] * (len(keys) + 2),
        out_specs=[in_vmem] * 3,
        out_shape=[
            jax.ShapeDtypeStruct((rows, columns), jnp.float32),
            jax.ShapeDtypeStruct((rows, columns), jnp.bfloat16),
            jax.ShapeDtypeStruct((PEERS, rows // LANES, LANES), jnp.float32),
        ],
        scratch_shapes=[pltpu.VMEM((2, rows, GROUP * width), jnp.bfloat16)],
        compiler_params=pltpu.CompilerParams(vmem_limit_bytes=HEAD_VMEM),
        name="head",
    )(*[blocks[key] for key in keys], early_squares(blocks), weight)


def gate_kernel(tops_ref, scores_ref, kept_ref, mass_ref):
    parts = tops_ref.shape[1]
    top = rows_of([jnp.max(tops_ref[:, part, :], axis=0, keepdims=True) for part in range(parts)])
    shifted = scores_ref[...] - top[:, :1]
    kept = jnp.exp(shifted) * jax.nn.sigmoid(gate_sharpness * (shifted - min_p_log))
    kept_ref[...] = kept
    spread_rows(jnp.sum(kept, axis=1, keepdims=True), mass_ref)


def gate(tops, scores):
    return pl.pallas_call(
        gate_kernel,
        out_shape=[
            jax.ShapeDtypeStruct(scores.shape, jnp.float32),
            jax.ShapeDtypeStruct(tops.shape, jnp.float32),
        ],
        compiler_params=pltpu.CompilerParams(vmem_limit_bytes=SMALL_VMEM),
        name="gate",
    )(tops, scores)


def share_kernel(masses_ref, kept_ref, probs_ref):
    parts = masses_ref.shape[1]
    mass = rows_of(
        [jnp.sum(masses_ref[:, part, :], axis=0, keepdims=True) for part in range(parts)]
    )
    probs_ref[...] = kept_ref[...] / mass[:, :1]


def share(masses, kept):
    return pl.pallas_call(
        share_kernel,
        out_shape=jax.ShapeDtypeStruct(kept.shape, jnp.float32),
        compiler_params=pltpu.CompilerParams(vmem_limit_bytes=SMALL_VMEM),
        name="share",
    )(masses, kept)


def local(hidden, norm_gain, head_weight):
    micro, rows, width = hidden.shape
    blocks = {}

    def keep(name, value):
        blocks[0, name] = value
        blocks[1, name] = fetch(value, 0, 0, 1)
        return value

    note = jnp.pad(norm_gain[None], ((0, NOTE - 1), (0, 0)))
    own = keep("own", jnp.concatenate([note, hidden.reshape(micro * rows, width)], axis=0))
    left, right = keep("left", fetch(own, 0, -1)), keep("right", fetch(own, 0, 1))
    down, up = keep("down", fetch(own, -1, 0)), keep("up", fetch(own, 1, 0))
    cross, over = keep("cross", fetch(own, 0, 2)), keep("over", fetch(own, 2, 0))

    row = join([left[:TOP], right[:TOP], cross[:TOP]])
    column = jnp.concatenate([down[TOP:], up[TOP:], over[TOP:]], axis=0)
    row_down, row_up = keep("row_down", fetch(row, -1, 0)), keep("row_up", fetch(row, 1, 0))
    col_left, col_right = (
        keep("col_left", fetch(column, 0, -1)),
        keep("col_right", fetch(column, 0, 1)),
    )
    keep("row_over", fetch(row, 2, 0))
    keep("col_cross", fetch(column, 0, 2))
    scores, logits, tops = head(blocks, head_weight)

    kept, masses = gate(exchange(tops), scores)
    probs = share(exchange(masses), kept)
    shape = (micro, rows, head_weight.shape[1])
    return logits.reshape(shape), probs.reshape(shape)


def solution(mesh):
    return jax.shard_map(
        local,
        mesh=mesh,
        in_specs=(
            P("dp", None, AXES),
            P(AXES),
            P(None, AXES),
        ),
        out_specs=(P("dp", None, AXES), P("dp", None, AXES)),
        check_vma=False,
    )
```
